32 devices in a mesh: dp: 8 (over z, x), tensor: 4 (over y, core).
Axes of the slice: x: 2, y: 2, z: 4, core: 2. Of those that a mesh axis runs over, the one named last changes fastest.
Arguments:
- tokens: bfloat16 [1024, 4096], P(('dp', 'tensor')), may hold values from -6 to 6
- query_base_weight: bfloat16 [4096, 4096], P(None, 'tensor'), may hold values from -0.09375 to 0.09375
- adapter_down_weight: bfloat16 [8, 16, 4096], P('dp', None, 'tensor'), may hold values from -0.09375 to 0.09375
- adapter_up_weight: bfloat16 [8, 16, 4096], P('dp', None, 'tensor'), may hold values from -0.375 to 0.375
- upstream: bfloat16 [1024, 4096], P('dp', 'tensor'), may hold values from -6 to 6
- adapter_per_block: int32 [8, 1], P('dp'), may hold values from 0 to 7
- owner: int32 [8], replicated, may hold values from 0 to 7, each once
Outputs:
- mixed: bfloat16 [1024, 4096], P('dp', 'tensor')
- input_gradient: bfloat16 [1024, 4096], P(('dp', 'tensor'))
- down_gradient: float32 [8, 16, 4096], P('dp', None, 'tensor')
- up_gradient: float32 [8, 16, 4096], P('dp', None, 'tensor')
The draws below stay inside these ranges and needn't reach their ends.
Inputs may be any that keep to these rules, and one draw needn't show every extreme that they name: `adapter_per_block`: every adapter has at least one block. `owner`: each slot is taken by exactly one adapter.
All inputs are finite; a program needn't handle non-finite values.
Results may differ from the reference program's by a relative error of at most 0.0032.
Values may be sent and summed in bfloat16 or wider, within the bound.
No kernel may reach another device: no remote copies, remote signals or barrier semaphores. Data moves between devices by JAX's collectives and lax.ppermute only.
A program may use at most 128 MiB of HBM per device.

```python
import jax
import jax.numpy as jnp
from jax import lax

MODEL_WIDTH = 4096
ADAPTER_RANK = 16
BLOCK = 128
ADAPTER_TOTAL = 8
BLOCKS = 8
TOKENS = 1024


def level_of(rng, shape, cuts, low, top_value):
    level = 1.0
    for dim, shards_of in cuts:
        steps = jax.random.uniform(jax.random.fold_in(jax.random.fold_in(rng, 6), dim), (shards_of,), jnp.float32, low / len(cuts), top_value / len(cuts))
        level = level * jnp.repeat(jnp.exp(steps), shape[dim] // shards_of).reshape((-1,) + (1,) * (len(shape) - 1 - dim))
    return level


def choose_distinct(stream_key, rows, count, top, lift):
    ranking = jax.random.permutation(jax.random.fold_in(stream_key, 1), count)
    favour = ranking
    for power in range(3):
        favour = favour * favour // count
    favour = favour * lift // count
    lots = jax.random.randint(jax.random.fold_in(stream_key, 2), (rows, count), 0, 4096) + favour
    sure = jax.random.permutation(jax.random.fold_in(stream_key, 3), rows)[jnp.arange(count) % rows]
    lots = jnp.where(jnp.arange(rows)[:, None] == sure[None, :], 1 << 14, lots)
    priority = lots * count + jnp.arange(count)
    return lax.top_k(priority.astype(jnp.int32), top)[1].astype(jnp.int32)


def centred(stream_key, extent, width, most, pieces=(), kind=jnp.bfloat16):
    level = level_of(stream_key, extent, pieces, -0.22, 0.18) if pieces else 1.0
    result = jax.random.normal(stream_key, extent, jnp.float32) * width * level
    return jnp.minimum(jnp.maximum(result, -most), most).astype(kind)


def setup_inputs(seed: int = 0) -> dict:
    key_list = jax.random.split(jax.random.key(seed), 8)
    return {
        "tokens": centred(key_list[0], (TOKENS, MODEL_WIDTH), 1.0, 6.0, ((0, 32),)),
        "query_base_weight": centred(key_list[1], (MODEL_WIDTH, MODEL_WIDTH), MODEL_WIDTH ** -0.5, 0.09375, ((1, 4),)),
        "adapter_down_weight": centred(key_list[2], (ADAPTER_TOTAL, ADAPTER_RANK, MODEL_WIDTH), MODEL_WIDTH ** -0.5, 0.09375, ((0, 8), (2, 4))),
        "adapter_up_weight": centred(key_list[3], (ADAPTER_TOTAL, ADAPTER_RANK, MODEL_WIDTH), (16 * ADAPTER_RANK) ** -0.5, 0.375, ((0, 8), (2, 4))),
        "upstream": centred(key_list[4], (TOKENS, MODEL_WIDTH), 1.0, 6.0, ((0, 8), (1, 4))),
        "adapter_per_block": choose_distinct(key_list[5], BLOCKS, ADAPTER_TOTAL, 1, 2048),
        "owner": jax.random.permutation(key_list[6], ADAPTER_TOTAL).astype(jnp.int32),
    }


adapter_scale = 2.0


def reference(tokens, query_base_weight, adapter_down_weight, adapter_up_weight, upstream, adapter_per_block, owner):
    slot_indices = owner[adapter_per_block[:, 0]]
    down_chosen = adapter_down_weight[slot_indices].astype(jnp.float32)
    up_chosen = adapter_up_weight[slot_indices].astype(jnp.float32)
    token_blocks = tokens.reshape(-1, BLOCK, MODEL_WIDTH).astype(jnp.float32)
    backward_blocks = upstream.reshape(-1, BLOCK, MODEL_WIDTH).astype(jnp.float32)
    reduced_hidden = jnp.einsum('mtn,myn->mty', token_blocks, down_chosen).astype(jnp.bfloat16)
    reduced_backward = jnp.einsum('mtn,myn->mty', backward_blocks, up_chosen).astype(jnp.bfloat16)
    reduced_function = reduced_hidden.astype(jnp.float32)
    backward_function = reduced_backward.astype(jnp.float32)
    mixed = jnp.dot(tokens, query_base_weight, preferred_element_type=jnp.float32)
    mixed = mixed + adapter_scale * jnp.einsum('xzv,xva->xza', reduced_function, up_chosen).reshape(-1, MODEL_WIDTH)
    input_gradient = jnp.dot(upstream, query_base_weight.T, preferred_element_type=jnp.float32)
    input_gradient = input_gradient + adapter_scale * jnp.einsum('xzv,xva->xza', backward_function, down_chosen).reshape(-1, MODEL_WIDTH)
    down_contributions = adapter_scale * jnp.einsum('phl,phj->plj', backward_function, token_blocks)
    up_contributions = adapter_scale * jnp.einsum('phl,phj->plj', reduced_function, backward_blocks)
    down_gradient = jax.ops.segment_sum(down_contributions, slot_indices, num_segments=ADAPTER_TOTAL)
    up_gradient = jax.ops.segment_sum(up_contributions, slot_indices, num_segments=ADAPTER_TOTAL)
    return mixed.astype(jnp.bfloat16), input_gradient.astype(jnp.bfloat16), down_gradient, up_gradient
```

```python
import functools

import jax
import jax.numpy as jnp
from jax import lax
from jax.experimental import pallas as pl
from jax.experimental.pallas import tpu as pltpu
from jax.sharding import PartitionSpec as P

adapter_scale = 2.0
bf16, f32 = jnp.bfloat16, jnp.float32
nt = (((1,), (1,)), ((), ()))
tn = (((0,), (0,)), ((), ()))
small_limit = 16 * 1024 * 1024
pieces_of_weight = 8
small_bytes = 8 * 1024 * 1024


def vmem():
    return pl.BlockSpec(memory_space=pltpu.VMEM)


def shape(dims, dtype):
    return jax.ShapeDtypeStruct(dims, dtype)


def call(
    body, name, outs, operands, specs, scratch=(), flops=0, moved=0, limit=small_limit, after=()
):
    count = len(operands)

    def run(*refs):
        body(*refs[:count], *refs[count + len(after) :])

    return list(
        pl.pallas_call(
            run,
            name=name,
            out_shape=outs,
            in_specs=specs + [pl.BlockSpec(memory_space=pl.ANY)] * len(after),
            out_specs=[vmem()] * len(outs),
            scratch_shapes=list(scratch),
            cost_estimate=pl.CostEstimate(flops=flops, bytes_accessed=moved, transcendentals=0),
            compiler_params=pltpu.CompilerParams(vmem_limit_bytes=limit),
        )(*operands, *after)
    )


def log2(n):
    return n.bit_length() - 1


def choose(refs, key):
    chosen = None
    for k in range(len(refs)):
        one = jnp.where(key == k, 1.0, 0.0).astype(bf16) * refs[k][...]
        chosen = one if chosen is None else chosen + one
    return chosen


def slot_kernel(*refs):
    owner, blocks = refs[0], refs[1:-5]
    tokens, upstream, slots, tokens_here, upstream_here = refs[-5:]
    tokens_here[...] = tokens[...]
    upstream_here[...] = upstream[...]
    adapters = lax.broadcasted_iota(jnp.int32, owner.shape, 1)
    for k in range(len(blocks)):
        here = jnp.where(adapters == blocks[k][...], owner[...], 0)
        slot = jnp.sum(here, axis=1, keepdims=True)
        slots[k : k + 1, :] = jnp.broadcast_to(slot, (1, slots.shape[1]))


def base_kernel(upstream, weight, keep, give, rows_of):
    t = lax.axis_index("tensor")
    rows = keep.shape[1]
    half = keep.shape[0]
    step = weight.shape[0] // pieces_of_weight
    for n in range(half):
        for side in range(2):
            start = pl.multiple_of((2 * n + ((t & 1) ^ side)) * rows, rows)
            at = (side * half + n) * rows
            rows_of[at : at + rows, :] = upstream[pl.ds(start, rows), :]
    for n in range(pieces_of_weight):
        part = lax.dot_general(rows_of[...], weight[n * step : (n + 1) * step, :], nt, preferred_element_type=f32)
        for m in range(half):
            keep[m, :, n * step : (n + 1) * step] = part[m * rows : (m + 1) * rows]
            at = (half + m) * rows
            give[m, :, n * step : (n + 1) * step] = part[at : at + rows]


def own_kernel(source, target):
    target[...] = source[...]


def pick_kernel(near, far, *refs):
    slots, group, found = refs[0], refs[1 : 1 + near], refs[1 + near :]
    i = lax.axis_index("dp") & (near - 1)
    for k in range(far):
        found[k][...] = choose(group, (slots[k : k + 1, :1] & (near - 1)) ^ i)


def low_kernel(near, far, parts, *refs):
    slots, found = refs[0], refs[1 : 1 + far]
    tokens = refs[1 + far : 1 + far + parts]
    upstream, both, chosen, columns, down = refs[1 + far + parts :]
    o = lax.axis_index("dp") >> log2(near)
    t = lax.axis_index("tensor")
    cols = columns.shape[1]
    rows = columns.shape[0] // parts
    rank = chosen.shape[0] // 2
    chosen[...] = choose(found, (slots[:1, :1] >> log2(near)) ^ o)
    down[...] = chosen[:rank, :]
    start = pl.multiple_of(t * cols, cols)
    for k in range(parts):
        at = pl.multiple_of((t ^ k) * rows, rows)
        columns[pl.ds(at, rows), :] = tokens[k][:, pl.ds(start, cols)]
    both[:rank, :] = lax.dot_general(
        chosen[:rank, :], columns[...], nt, preferred_element_type=f32
    )
    both[rank:, :] = lax.dot_general(
        chosen[rank:, :], upstream[...], nt, preferred_element_type=f32
    )


def gradient_kernel(parts, *refs):
    totals = refs[:parts]
    columns, upstream, low, term = refs[parts:]
    rank = low.shape[0] // 2
    total = totals[0][...]
    for k in range(1, parts):
        total = total + totals[k][...]
    low[...] = total.astype(bf16)
    down_term = jnp.dot(low[rank:, :], columns[...], preferred_element_type=f32)
    up_term = jnp.dot(low[:rank, :], upstream[...], preferred_element_type=f32)
    term[:rank, :] = (adapter_scale * down_term).astype(bf16)
    term[rank:, :] = (adapter_scale * up_term).astype(bf16)


def route_kernel(near, far, *refs):
    slots, terms, parts = refs[0], refs[1 : 1 + far], refs[1 + far :]
    d = lax.axis_index("dp")
    for m in range(near):
        part = None
        for k in range(far):
            here = jnp.where(slots[k : k + 1, :1] == (d ^ m), 1.0, 0.0).astype(bf16)
            one = here * terms[k][...]
            part = one if part is None else part + one
        parts[m][...] = part


def add_kernel(keep, got, low, chosen, sibling, hold, give, total, term):
    t = lax.axis_index("tensor")
    half, rows = keep.shape[0], keep.shape[1]
    rank, cols = sibling.shape
    high = t >> 1
    total[...] = keep[...] + got[...]
    for k, down in ((0, chosen), (1, sibling)):
        term[...] = adapter_scale * lax.dot_general(
            low[rank:, :], down[:rank, :], tn, preferred_element_type=f32
        )
        at = pl.multiple_of((t ^ k) * cols, cols)
        for n in range(half):
            start = pl.multiple_of((2 * n + (t & 1)) * rows, rows)
            total[n, :, pl.ds(at, cols)] += term[pl.ds(start, rows), :]
    hold[...] = total[high]
    give[...] = total[1 - high].astype(bf16)


def mixed_kernel(parts, *refs):
    tokens = refs[:parts]
    weight, total, gathered = refs[parts:]
    t = lax.axis_index("tensor")
    rows = tokens[0].shape[0]
    step = weight.shape[0] // pieces_of_weight
    for k in range(parts):
        at = pl.multiple_of((t ^ k) * rows, rows)
        gathered[pl.ds(at, rows), :] = tokens[k][...]
    for n in range(pieces_of_weight):
        part = jnp.dot(
            gathered[:, n * step : (n + 1) * step],
            weight[n * step : (n + 1) * step, :],
            preferred_element_type=f32,
        )
        total[...] = part if n == 0 else total[...] + part


def finish_kernel(mixed, low, chosen, out):
    rank = low.shape[0] // 2
    term = lax.dot_general(low[:rank, :], chosen[rank:, :], tn, preferred_element_type=f32)
    out[...] = (mixed[...] + adapter_scale * term).astype(bf16)


def close_kernel(hold, got, out, done):
    out[...] = (hold[...] + got[...].astype(f32)).astype(bf16)
    done[...] = jnp.zeros(done.shape, f32)


def sum_kernel(*refs):
    parts, down, up = refs[:-2], refs[-2], refs[-1]
    rank = down.shape[1]
    total = parts[0][...].astype(f32)
    for part in parts[1:]:
        total = total + part[...].astype(f32)
    down[0] = total[:rank, :]
    up[0] = total[rank:, :]


def make_per_device(dp_size, tensor_size):
    near = 1 << ((log2(dp_size) + 1) // 2)
    far = dp_size // near
    half = tensor_size // 2

    def over_tensor(x, k):
        return lax.ppermute(x, "tensor", [(t, t ^ k) for t in range(tensor_size)])

    def over_near(x, k):
        return lax.ppermute(x, "dp", [(d, d ^ k) for d in range(dp_size)])

    def over_far(x, k):
        return lax.ppermute(x, "dp", [(d, d ^ (k * near)) for d in range(dp_size)])

    def per_device(tokens, weight, down, up, upstream, adapter_per_block, owner):
        rank, cols = down.shape[1], down.shape[2]
        rows, width = tokens.shape
        length = upstream.shape[0]
        weight_bytes = weight.shape[0] * cols * 2
        flops = 2 * length * weight.shape[0] * cols

        mine = jnp.concatenate([down[0], up[0]], axis=0)
        group = [mine] + [over_near(mine, k) for k in range(1, near)]
        across = over_tensor(tokens, half)
        blocks = [adapter_per_block]
        blocks += [over_far(adapter_per_block, k) for k in range(1, far)]

        (group[0],) = call(
            own_kernel,
            "own",
            [shape(mine.shape, bf16)],
            (mine,),
            [vmem()],
            flops=8 * flops,
            after=(across, *blocks[1:]),
        )
        slots, tokens_here, upstream_here = call(
            slot_kernel,
            "slots",
            [
                shape((far, 128), jnp.int32),
                shape(tokens.shape, bf16),
                shape(upstream.shape, bf16),
            ],
            (owner.reshape(1, -1), *blocks, tokens, upstream),
            [vmem()] * (far + 3),
            flops=flops,
            moved=small_bytes,
            after=(group[0],),
        )
        pieces = [tokens_here, over_tensor(tokens_here, 1), across, over_tensor(across, 1)]
        found = call(
            functools.partial(pick_kernel, near, far),
            "pick",
            [shape((2 * rank, cols), bf16)] * far,
            (slots, *group),
            [vmem()] * (1 + near),
            flops=flops,
            moved=small_bytes,
        )
        keep, give = call(
            base_kernel,
            "base",
            [shape((half, rows, width), f32)] * 2,
            (upstream_here, weight),
            [vmem(), vmem()],
            [pltpu.VMEM((length, cols), bf16)],
            flops,
            weight_bytes,
            after=(found[0],),
        )
        found = [found[0]] + [over_far(found[k], k) for k in range(1, far)]

        both, chosen, columns, chosen_down = call(
            functools.partial(low_kernel, near, far, tensor_size),
            "low",
            [
                shape((2 * rank, length), f32),
                shape((2 * rank, cols), bf16),
                shape((length, cols), bf16),
                shape((rank, cols), bf16),
            ],
            (slots, *found, *pieces, upstream_here),
            [vmem()] * (1 + far + tensor_size + 1),
            flops=flops,
            moved=small_bytes,
        )
        (mixed,) = call(
            functools.partial(mixed_kernel, tensor_size),
            "mixed",
            [shape((length, cols), f32)],
            (*pieces, weight),
            [vmem()] * (tensor_size + 1),
            [pltpu.VMEM((length, width), bf16)],
            flops,
            weight_bytes,
            after=(both,),
        )
        give, both = lax.optimization_barrier((give, both))
        got = over_tensor(give, 1)
        sibling = over_tensor(chosen_down, 1)
        totals = [both] + [over_tensor(both, k) for k in range(1, tensor_size)]

        low, term = call(
            functools.partial(gradient_kernel, tensor_size),
            "gradient",
            [shape((2 * rank, length), bf16), shape((2 * rank, cols), bf16)],
            (*totals, columns, upstream_here),
            [vmem()] * (tensor_size + 2),
            after=(mixed, sibling),
        )
        terms = [term] + [over_far(term, k) for k in range(1, far)]

        hold, give = call(
            add_kernel,
            "add",
            [shape((rows, width), f32), shape((rows, width), bf16)],
            (keep, got, low, chosen, sibling),
            [vmem()] * 5,
            [pltpu.VMEM((half, rows, width), f32), pltpu.VMEM((length, cols), f32)],
        )
        got = over_tensor(give, half)

        routed = call(
            functools.partial(route_kernel, near, far),
            "route",
            [shape((2 * rank, cols), bf16)] * near,
            (slots, *terms),
            [vmem()] * (1 + far),
            after=(give,),
        )
        parts = [routed[0]] + [over_near(routed[m], m) for m in range(1, near)]
        (mixed,) = call(
            finish_kernel,
            "finish",
            [shape((length, cols), bf16)],
            (mixed, low, chosen),
            [vmem()] * 3,
            flops=4 * flops,
            after=(routed[0],),
        )
        input_gradient, done = call(
            close_kernel,
            "close",
            [shape((rows, width), bf16), shape((8, 128), f32)],
            (hold, got),
            [vmem()] * 2,
        )
        down_gradient, up_gradient = call(
            sum_kernel,
            "sum",
            [shape(down.shape, f32)] * 2,
            parts,
            [vmem()] * near,
            after=(done,),
        )
        return mixed, input_gradient, down_gradient, up_gradient

    return per_device


def solution(mesh):
    return jax.shard_map(
        make_per_device(mesh.shape["dp"], mesh.shape["tensor"]),
        mesh=mesh,
        in_specs=(
            P(("dp", "tensor"), None),
            P(None, "tensor"),
            P("dp", None, "tensor"),
            P("dp", None, "tensor"),
            P("dp", "tensor"),
            P("dp", None),
            P(),
        ),
        out_specs=(
            P("dp", "tensor"),
            P(("dp", "tensor"), None),
            P("dp", None, "tensor"),
            P("dp", None, "tensor"),
        ),
        check_vma=False,
    )
```

```python
import functools

import jax
import jax.numpy as jnp
from jax import lax
from jax.experimental import pallas as pl
from jax.experimental.pallas import tpu as pltpu
from jax.sharding import PartitionSpec as P

adapter_scale = 2.0
bf16, f32 = jnp.bfloat16, jnp.float32
nt = (((1,), (1,)), ((), ()))
tn = (((0,), (0,)), ((), ()))
small_limit = 16 * 1024 * 1024
pieces_of_weight = 8
small_bytes = 8 * 1024 * 1024


def vmem():
    return pl.BlockSpec(memory_space=pltpu.VMEM)


def shape(dims, dtype):
    return jax.ShapeDtypeStruct(dims, dtype)


def call(
    body, name, outs, operands, specs, scratch=(), flops=0, moved=0, limit=small_limit, after=()
):
    count = len(operands)

    def run(*refs):
        body(*refs[:count], *refs[count + len(after) :])

    return list(
        pl.pallas_call(
            run,
            name=name,
            out_shape=outs,
            in_specs=specs + [pl.BlockSpec(memory_space=pl.ANY)] * len(after),
            out_specs=[vmem()] * len(outs),
            scratch_shapes=list(scratch),
            cost_estimate=pl.CostEstimate(flops=flops, bytes_accessed=moved, transcendentals=0),
            compiler_params=pltpu.CompilerParams(vmem_limit_bytes=limit),
        )(*operands, *after)
    )


def log2(n):
    return n.bit_length() - 1


def choose(refs, key):
    chosen = None
    for k in range(len(refs)):
        one = jnp.where(key == k, 1.0, 0.0).astype(bf16) * refs[k][...]
        chosen = one if chosen is None else chosen + one
    return chosen


def slot_kernel(*refs):
    owner, blocks = refs[0], refs[1:-5]
    tokens, upstream, slots, tokens_here, upstream_here = refs[-5:]
    tokens_here[...] = tokens[...]
    upstream_here[...] = upstream[...]
    adapters = lax.broadcasted_iota(jnp.int32, owner.shape, 1)
    for k in range(len(blocks)):
        here = jnp.where(adapters == blocks[k][...], owner[...], 0)
        slot = jnp.sum(here, axis=1, keepdims=True)
        slots[k : k + 1, :] = jnp.broadcast_to(slot, (1, slots.shape[1]))


def base_kernel(upstream, weight, keep, give, rows_of):
    t = lax.axis_index("tensor")
    rows = keep.shape[1]
    half = keep.shape[0]
    step = weight.shape[0] // pieces_of_weight
    for n in range(half):
        for side in range(2):
            start = pl.multiple_of((2 * n + ((t & 1) ^ side)) * rows, rows)
            at = (side * half + n) * rows
            rows_of[at : at + rows, :] = upstream[pl.ds(start, rows), :]
    for n in range(pieces_of_weight):
        part = lax.dot_general(rows_of[...], weight[n * step : (n + 1) * step, :], nt, preferred_element_type=f32)
        for m in range(half):
            keep[m, :, n * step : (n + 1) * step] = part[m * rows : (m + 1) * rows]
            at = (half + m) * rows
            give[m, :, n * step : (n + 1) * step] = part[at : at + rows]


def own_kernel(source, target):
    target[...] = source[...]


def pick_kernel(outer, inner, *refs):
    slots, column, found = refs[0], refs[1 : 1 + outer], refs[1 + outer :]
    o = lax.axis_index("dp") >> log2(inner)
    for k in range(inner):
        found[k][...] = choose(column, (slots[k : k + 1, :1] >> log2(inner)) ^ o)


def low_kernel(inner, parts, *refs):
    slots, found = refs[0], refs[1 : 1 + inner]
    tokens = refs[1 + inner : 1 + inner + parts]
    upstream, both, chosen, columns, down = refs[1 + inner + parts :]
    i = lax.axis_index("dp") & (inner - 1)
    t = lax.axis_index("tensor")
    cols = columns.shape[1]
    rows = columns.shape[0] // parts
    rank = chosen.shape[0] // 2
    chosen[...] = choose(found, (slots[:1, :1] & (inner - 1)) ^ i)
    down[...] = chosen[:rank, :]
    start = pl.multiple_of(t * cols, cols)
    for k in range(parts):
        at = pl.multiple_of((t ^ k) * rows, rows)
        columns[pl.ds(at, rows), :] = tokens[k][:, pl.ds(start, cols)]
    both[:rank, :] = lax.dot_general(
        chosen[:rank, :], columns[...], nt, preferred_element_type=f32
    )
    both[rank:, :] = lax.dot_general(
        chosen[rank:, :], upstream[...], nt, preferred_element_type=f32
    )


def gradient_kernel(parts, *refs):
    totals = refs[:parts]
    columns, upstream, low, term = refs[parts:]
    rank = low.shape[0] // 2
    total = totals[0][...]
    for k in range(1, parts):
        total = total + totals[k][...]
    low[...] = total.astype(bf16)
    down_term = jnp.dot(low[rank:, :], columns[...], preferred_element_type=f32)
    up_term = jnp.dot(low[:rank, :], upstream[...], preferred_element_type=f32)
    term[:rank, :] = (adapter_scale * down_term).astype(bf16)
    term[rank:, :] = (adapter_scale * up_term).astype(bf16)


def route_kernel(outer, inner, *refs):
    slots, terms, parts = refs[0], refs[1 : 1 + inner], refs[1 + inner :]
    d = lax.axis_index("dp")
    for m in range(outer):
        target = d ^ (m * inner)
        part = None
        for k in range(inner):
            here = jnp.where(slots[k : k + 1, :1] == target, 1.0, 0.0).astype(bf16)
            one = here * terms[k][...]
            part = one if part is None else part + one
        parts[m][...] = part


def add_kernel(keep, got, low, chosen, sibling, hold, give, total, term):
    t = lax.axis_index("tensor")
    half, rows = keep.shape[0], keep.shape[1]
    rank, cols = sibling.shape
    high = t >> 1
    total[...] = keep[...] + got[...]
    for k, down in ((0, chosen), (1, sibling)):
        term[...] = adapter_scale * lax.dot_general(
            low[rank:, :], down[:rank, :], tn, preferred_element_type=f32
        )
        at = pl.multiple_of((t ^ k) * cols, cols)
        for n in range(half):
            start = pl.multiple_of((2 * n + (t & 1)) * rows, rows)
            total[n, :, pl.ds(at, cols)] += term[pl.ds(start, rows), :]
    hold[...] = total[high]
    give[...] = total[1 - high].astype(bf16)


def mixed_kernel(parts, *refs):
    tokens = refs[:parts]
    weight, total, gathered = refs[parts:]
    t = lax.axis_index("tensor")
    rows = tokens[0].shape[0]
    step = weight.shape[0] // pieces_of_weight
    for k in range(parts):
        at = pl.multiple_of((t ^ k) * rows, rows)
        gathered[pl.ds(at, rows), :] = tokens[k][...]
    for n in range(pieces_of_weight):
        part = jnp.dot(
            gathered[:, n * step : (n + 1) * step],
            weight[n * step : (n + 1) * step, :],
            preferred_element_type=f32,
        )
        total[...] = part if n == 0 else total[...] + part


def finish_kernel(mixed, low, chosen, out):
    rank = low.shape[0] // 2
    term = lax.dot_general(low[:rank, :], chosen[rank:, :], tn, preferred_element_type=f32)
    out[...] = (mixed[...] + adapter_scale * term).astype(bf16)


def close_kernel(hold, got, out, done):
    out[...] = (hold[...] + got[...].astype(f32)).astype(bf16)
    done[...] = jnp.zeros(done.shape, f32)


def sum_kernel(*refs):
    parts, down, up = refs[:-2], refs[-2], refs[-1]
    rank = down.shape[1]
    total = parts[0][...].astype(f32)
    for part in parts[1:]:
        total = total + part[...].astype(f32)
    down[0] = total[:rank, :]
    up[0] = total[rank:, :]


def make_per_device(dp_size, tensor_size):
    inner = 1 << (log2(dp_size) // 2)
    outer = dp_size // inner
    half = tensor_size // 2

    def over_tensor(x, k):
        return lax.ppermute(x, "tensor", [(t, t ^ k) for t in range(tensor_size)])

    def over_inner(x, k):
        return lax.ppermute(x, "dp", [(d, d ^ k) for d in range(dp_size)])

    def over_outer(x, k):
        return lax.ppermute(x, "dp", [(d, d ^ (k * inner)) for d in range(dp_size)])

    def per_device(tokens, weight, down, up, upstream, adapter_per_block, owner):
        rank, cols = down.shape[1], down.shape[2]
        rows, width = tokens.shape
        length = upstream.shape[0]
        weight_bytes = weight.shape[0] * cols * 2
        flops = 2 * length * weight.shape[0] * cols

        mine = jnp.concatenate([down[0], up[0]], axis=0)
        column = [mine] + [over_outer(mine, k) for k in range(1, outer)]
        far = over_tensor(tokens, half)
        blocks = [adapter_per_block]
        blocks += [over_inner(adapter_per_block, k) for k in range(1, inner)]

        (column[0],) = call(
            own_kernel,
            "own",
            [shape(mine.shape, bf16)],
            (mine,),
            [vmem()],
            flops=8 * flops,
            after=(far,),
        )
        slots, tokens_here, upstream_here = call(
            slot_kernel,
            "slots",
            [
                shape((inner, 128), jnp.int32),
                shape(tokens.shape, bf16),
                shape(upstream.shape, bf16),
            ],
            (owner.reshape(1, -1), *blocks, tokens, upstream),
            [vmem()] * (inner + 3),
            flops=flops,
            moved=small_bytes,
            after=(column[0],),
        )
        pieces = [tokens_here, over_tensor(tokens_here, 1), far, over_tensor(far, 1)]
        found = call(
            functools.partial(pick_kernel, outer, inner),
            "pick",
            [shape((2 * rank, cols), bf16)] * inner,
            (slots, *column),
            [vmem()] * (1 + outer),
            flops=flops,
            moved=small_bytes,
        )
        keep, give = call(
            base_kernel,
            "base",
            [shape((half, rows, width), f32)] * 2,
            (upstream_here, weight),
            [vmem(), vmem()],
            [pltpu.VMEM((length, cols), bf16)],
            flops,
            weight_bytes,
            after=(found[0],),
        )
        found = [found[0]] + [over_inner(found[k], k) for k in range(1, inner)]

        both, chosen, columns, chosen_down = call(
            functools.partial(low_kernel, inner, tensor_size),
            "low",
            [
                shape((2 * rank, length), f32),
                shape((2 * rank, cols), bf16),
                shape((length, cols), bf16),
                shape((rank, cols), bf16),
            ],
            (slots, *found, *pieces, upstream_here),
            [vmem()] * (1 + inner + tensor_size + 1),
            flops=flops,
            moved=small_bytes,
        )
        (mixed,) = call(
            functools.partial(mixed_kernel, tensor_size),
            "mixed",
            [shape((length, cols), f32)],
            (*pieces, weight),
            [vmem()] * (tensor_size + 1),
            [pltpu.VMEM((length, width), bf16)],
            flops,
            weight_bytes,
            after=(both,),
        )
        give, both = lax.optimization_barrier((give, both))
        got = over_tensor(give, 1)
        sibling = over_tensor(chosen_down, 1)
        totals = [both] + [over_tensor(both, k) for k in range(1, tensor_size)]

        low, term = call(
            functools.partial(gradient_kernel, tensor_size),
            "gradient",
            [shape((2 * rank, length), bf16), shape((2 * rank, cols), bf16)],
            (*totals, columns, upstream_here),
            [vmem()] * (tensor_size + 2),
            after=(mixed, sibling),
        )
        terms = [term] + [over_inner(term, k) for k in range(1, inner)]

        hold, give = call(
            add_kernel,
            "add",
            [shape((rows, width), f32), shape((rows, width), bf16)],
            (keep, got, low, chosen, sibling),
            [vmem()] * 5,
            [pltpu.VMEM((half, rows, width), f32), pltpu.VMEM((length, cols), f32)],
        )
        got = over_tensor(give, half)

        routed = call(
            functools.partial(route_kernel, outer, inner),
            "route",
            [shape((2 * rank, cols), bf16)] * outer,
            (slots, *terms),
            [vmem()] * (1 + inner),
            after=(give,),
        )
        parts = [routed[0]] + [over_outer(routed[m], m) for m in range(1, outer)]
        (mixed,) = call(
            finish_kernel,
            "finish",
            [shape((length, cols), bf16)],
            (mixed, low, chosen),
            [vmem()] * 3,
            flops=4 * flops,
            after=(routed[0],),
        )
        input_gradient, done = call(
            close_kernel,
            "close",
            [shape((rows, width), bf16), shape((8, 128), f32)],
            (hold, got),
            [vmem()] * 2,
        )
        down_gradient, up_gradient = call(
            sum_kernel,
            "sum",
            [shape(down.shape, f32)] * 2,
            parts[:1] + parts[:0:-1],
            [vmem()] * outer,
            after=(done,),
        )
        return mixed, input_gradient, down_gradient, up_gradient

    return per_device


def solution(mesh):
    return jax.shard_map(
        make_per_device(mesh.shape["dp"], mesh.shape["tensor"]),
        mesh=mesh,
        in_specs=(
            P(("dp", "tensor"), None),
            P(None, "tensor"),
            P("dp", None, "tensor"),
            P("dp", None, "tensor"),
            P("dp", "tensor"),
            P("dp", None),
            P(),
        ),
        out_specs=(
            P("dp", "tensor"),
            P(("dp", "tensor"), None),
            P("dp", None, "tensor"),
            P("dp", None, "tensor"),
        ),
        check_vma=False,
    )
```

```python
import functools

import jax
import jax.numpy as jnp
from jax import lax
from jax.experimental import pallas as pl
from jax.experimental.pallas import tpu as pltpu
from jax.sharding import PartitionSpec as P

adapter_scale = 2.0
bf16, f32 = jnp.bfloat16, jnp.float32
nt = (((1,), (1,)), ((), ()))
tn = (((0,), (0,)), ((), ()))
small_limit = 16 * 1024 * 1024
pieces_of_weight = 8
small_bytes = 8 * 1024 * 1024


def vmem():
    return pl.BlockSpec(memory_space=pltpu.VMEM)


def shape(dims, dtype):
    return jax.ShapeDtypeStruct(dims, dtype)


def call(
    body, name, outs, operands, specs, scratch=(), flops=0, moved=0, limit=small_limit, after=()
):
    count = len(operands)

    def run(*refs):
        body(*refs[:count], *refs[count + len(after) :])

    return list(
        pl.pallas_call(
            run,
            name=name,
            out_shape=outs,
            in_specs=specs + [pl.BlockSpec(memory_space=pl.ANY)] * len(after),
            out_specs=[vmem()] * len(outs),
            scratch_shapes=list(scratch),
            cost_estimate=pl.CostEstimate(flops=flops, bytes_accessed=moved, transcendentals=0),
            compiler_params=pltpu.CompilerParams(vmem_limit_bytes=limit),
        )(*operands, *after)
    )


def log2(n):
    return n.bit_length() - 1


def choose(refs, key):
    chosen = None
    for k in range(len(refs)):
        one = jnp.where(key == k, 1.0, 0.0).astype(bf16) * refs[k][...]
        chosen = one if chosen is None else chosen + one
    return chosen


def slot_kernel(*refs):
    owner, blocks = refs[0], refs[1:-5]
    tokens, upstream, slots, tokens_here, upstream_here = refs[-5:]
    tokens_here[...] = tokens[...]
    upstream_here[...] = upstream[...]
    adapters = lax.broadcasted_iota(jnp.int32, owner.shape, 1)
    for k in range(len(blocks)):
        here = jnp.where(adapters == blocks[k][:1, :1], owner[...], 0)
        slot = jnp.sum(here, axis=1, keepdims=True)
        slots[k : k + 1, :] = jnp.broadcast_to(slot, (1, slots.shape[1]))


def base_kernel(upstream, weight, keep, give, rows_of):
    t = lax.axis_index("tensor")
    rows = keep.shape[1]
    half = keep.shape[0]
    step = weight.shape[0] // pieces_of_weight
    for n in range(half):
        for side in range(2):
            start = pl.multiple_of((2 * n + ((t & 1) ^ side)) * rows, rows)
            at = (side * half + n) * rows
            rows_of[at : at + rows, :] = upstream[pl.ds(start, rows), :]
    for n in range(pieces_of_weight):
        part = lax.dot_general(rows_of[...], weight[n * step : (n + 1) * step, :], nt, preferred_element_type=f32)
        for m in range(half):
            keep[m, :, n * step : (n + 1) * step] = part[m * rows : (m + 1) * rows]
            at = (half + m) * rows
            give[m, :, n * step : (n + 1) * step] = part[at : at + rows]


def own_kernel(source, target):
    target[...] = source[...]


def pick_kernel(outer, inner, *refs):
    slots, column, found = refs[0], refs[1 : 1 + outer], refs[1 + outer :]
    o = lax.axis_index("dp") >> log2(inner)
    for k in range(inner):
        found[k][...] = choose(column, (slots[k : k + 1, :1] >> log2(inner)) ^ o)


def low_kernel(inner, parts, *refs):
    slots, found = refs[0], refs[1 : 1 + inner]
    tokens = refs[1 + inner : 1 + inner + parts]
    upstream, both, chosen, columns, down = refs[1 + inner + parts :]
    i = lax.axis_index("dp") & (inner - 1)
    t = lax.axis_index("tensor")
    cols = columns.shape[1]
    rows = columns.shape[0] // parts
    rank = chosen.shape[0] // 2
    chosen[...] = choose(found, (slots[:1, :1] & (inner - 1)) ^ i)
    down[...] = chosen[:rank, :]
    start = pl.multiple_of(t * cols, cols)
    for k in range(parts):
        at = pl.multiple_of((t ^ k) * rows, rows)
        columns[pl.ds(at, rows), :] = tokens[k][:, pl.ds(start, cols)]
    both[:rank, :] = lax.dot_general(
        chosen[:rank, :], columns[...], nt, preferred_element_type=f32
    )
    both[rank:, :] = lax.dot_general(
        chosen[rank:, :], upstream[...], nt, preferred_element_type=f32
    )


def gradient_kernel(parts, *refs):
    totals = refs[:parts]
    columns, upstream, low, term = refs[parts:]
    rank = low.shape[0] // 2
    total = totals[0][...]
    for k in range(1, parts):
        total = total + totals[k][...]
    low[...] = total.astype(bf16)
    down_term = jnp.dot(low[rank:, :], columns[...], preferred_element_type=f32)
    up_term = jnp.dot(low[:rank, :], upstream[...], preferred_element_type=f32)
    term[:rank, :] = (adapter_scale * down_term).astype(bf16)
    term[rank:, :] = (adapter_scale * up_term).astype(bf16)


def route_kernel(outer, inner, *refs):
    slots, terms, parts = refs[0], refs[1 : 1 + inner], refs[1 + inner :]
    d = lax.axis_index("dp")
    for m in range(outer):
        target = d ^ (m * inner)
        part = None
        for k in range(inner):
            here = jnp.where(slots[k : k + 1, :1] == target, 1.0, 0.0).astype(bf16)
            one = here * terms[k][...]
            part = one if part is None else part + one
        parts[m][...] = part


def add_kernel(keep, got, low, chosen, sibling, hold, give, total, term):
    t = lax.axis_index("tensor")
    half, rows = keep.shape[0], keep.shape[1]
    rank, cols = sibling.shape
    high = t >> 1
    total[...] = keep[...] + got[...]
    for k, down in ((0, chosen), (1, sibling)):
        term[...] = adapter_scale * lax.dot_general(
            low[rank:, :], down[:rank, :], tn, preferred_element_type=f32
        )
        at = pl.multiple_of((t ^ k) * cols, cols)
        for n in range(half):
            start = pl.multiple_of((2 * n + (t & 1)) * rows, rows)
            total[n, :, pl.ds(at, cols)] += term[pl.ds(start, rows), :]
    hold[...] = total[high]
    give[...] = total[1 - high].astype(bf16)


def mixed_kernel(parts, *refs):
    tokens = refs[:parts]
    weight, total, gathered = refs[parts:]
    t = lax.axis_index("tensor")
    rows = tokens[0].shape[0]
    step = weight.shape[0] // pieces_of_weight
    for k in range(parts):
        at = pl.multiple_of((t ^ k) * rows, rows)
        gathered[pl.ds(at, rows), :] = tokens[k][...]
    for n in range(pieces_of_weight):
        part = jnp.dot(
            gathered[:, n * step : (n + 1) * step],
            weight[n * step : (n + 1) * step, :],
            preferred_element_type=f32,
        )
        total[...] = part if n == 0 else total[...] + part


def finish_kernel(mixed, low, chosen, out):
    rank = low.shape[0] // 2
    term = lax.dot_general(low[:rank, :], chosen[rank:, :], tn, preferred_element_type=f32)
    out[...] = (mixed[...] + adapter_scale * term).astype(bf16)


def close_kernel(hold, got, out, done):
    out[...] = (hold[...] + got[...].astype(f32)).astype(bf16)
    done[...] = jnp.zeros(done.shape, f32)


def sum_kernel(*refs):
    parts, down, up = refs[:-2], refs[-2], refs[-1]
    rank = down.shape[1]
    total = parts[0][...].astype(f32)
    for part in parts[1:]:
        total = total + part[...].astype(f32)
    down[0] = total[:rank, :]
    up[0] = total[rank:, :]


def make_per_device(dp_size, tensor_size):
    inner = 1 << (log2(dp_size) // 2)
    outer = dp_size // inner
    half = tensor_size // 2

    def over_tensor(x, k):
        return lax.ppermute(x, "tensor", [(t, t ^ k) for t in range(tensor_size)])

    def over_inner(x, k):
        return lax.ppermute(x, "dp", [(d, d ^ k) for d in range(dp_size)])

    def over_outer(x, k):
        return lax.ppermute(x, "dp", [(d, d ^ (k * inner)) for d in range(dp_size)])

    def per_device(tokens, weight, down, up, upstream, adapter_per_block, owner):
        rank, cols = down.shape[1], down.shape[2]
        rows, width = tokens.shape
        length = upstream.shape[0]
        weight_bytes = weight.shape[0] * cols * 2
        flops = 2 * length * weight.shape[0] * cols

        mine = jnp.concatenate([down[0], up[0]], axis=0)
        column = [mine] + [over_outer(mine, k) for k in range(1, outer)]
        far = over_tensor(tokens, half)
        block = jnp.broadcast_to(adapter_per_block, (8, 128))
        blocks = [block] + [over_inner(block, k) for k in range(1, inner)]

        (column[0],) = call(
            own_kernel,
            "own",
            [shape(mine.shape, bf16)],
            (mine,),
            [vmem()],
            flops=8 * flops,
            after=(far,),
        )
        slots, tokens_here, upstream_here = call(
            slot_kernel,
            "slots",
            [
                shape((inner, 128), jnp.int32),
                shape(tokens.shape, bf16),
                shape(upstream.shape, bf16),
            ],
            (owner.reshape(1, -1), *blocks, tokens, upstream),
            [vmem()] * (inner + 3),
            flops=flops,
            moved=small_bytes,
            after=(column[0],),
        )
        pieces = [tokens_here, over_tensor(tokens_here, 1), far, over_tensor(far, 1)]
        found = call(
            functools.partial(pick_kernel, outer, inner),
            "pick",
            [shape((2 * rank, cols), bf16)] * inner,
            (slots, *column),
            [vmem()] * (1 + outer),
            flops=flops,
            moved=small_bytes,
        )
        keep, give = call(
            base_kernel,
            "base",
            [shape((half, rows, width), f32)] * 2,
            (upstream_here, weight),
            [vmem(), vmem()],
            [pltpu.VMEM((length, cols), bf16)],
            flops,
            weight_bytes,
            after=(found[0],),
        )
        found = [found[0]] + [over_inner(found[k], k) for k in range(1, inner)]

        both, chosen, columns, chosen_down = call(
            functools.partial(low_kernel, inner, tensor_size),
            "low",
            [
                shape((2 * rank, length), f32),
                shape((2 * rank, cols), bf16),
                shape((length, cols), bf16),
                shape((rank, cols), bf16),
            ],
            (slots, *found, *pieces, upstream_here),
            [vmem()] * (1 + inner + tensor_size + 1),
            flops=flops,
            moved=small_bytes,
        )
        (mixed,) = call(
            functools.partial(mixed_kernel, tensor_size),
            "mixed",
            [shape((length, cols), f32)],
            (*pieces, weight),
            [vmem()] * (tensor_size + 1),
            [pltpu.VMEM((length, width), bf16)],
            flops,
            weight_bytes,
            after=(both,),
        )
        give, both = lax.optimization_barrier((give, both))
        got = over_tensor(give, 1)
        sibling = over_tensor(chosen_down, 1)
        totals = [both] + [over_tensor(both, k) for k in range(1, tensor_size)]

        low, term = call(
            functools.partial(gradient_kernel, tensor_size),
            "gradient",
            [shape((2 * rank, length), bf16), shape((2 * rank, cols), bf16)],
            (*totals, columns, upstream_here),
            [vmem()] * (tensor_size + 2),
            after=(mixed, sibling),
        )
        terms = [term] + [over_inner(term, k) for k in range(1, inner)]

        hold, give = call(
            add_kernel,
            "add",
            [shape((rows, width), f32), shape((rows, width), bf16)],
            (keep, got, low, chosen, sibling),
            [vmem()] * 5,
            [pltpu.VMEM((half, rows, width), f32), pltpu.VMEM((length, cols), f32)],
        )
        got = over_tensor(give, half)

        routed = call(
            functools.partial(route_kernel, outer, inner),
            "route",
            [shape((2 * rank, cols), bf16)] * outer,
            (slots, *terms),
            [vmem()] * (1 + inner),
            after=(give,),
        )
        parts = [routed[0]] + [over_outer(routed[m], m) for m in range(1, outer)]
        (mixed,) = call(
            finish_kernel,
            "finish",
            [shape((length, cols), bf16)],
            (mixed, low, chosen),
            [vmem()] * 3,
            flops=4 * flops,
            after=(routed[0],),
        )
        input_gradient, done = call(
            close_kernel,
            "close",
            [shape((rows, width), bf16), shape((8, 128), f32)],
            (hold, got),
            [vmem()] * 2,
        )
        down_gradient, up_gradient = call(
            sum_kernel,
            "sum",
            [shape(down.shape, f32)] * 2,
            parts[:1] + parts[:0:-1],
            [vmem()] * outer,
            after=(done,),
        )
        return mixed, input_gradient, down_gradient, up_gradient

    return per_device


def solution(mesh):
    return jax.shard_map(
        make_per_device(mesh.shape["dp"], mesh.shape["tensor"]),
        mesh=mesh,
        in_specs=(
            P(("dp", "tensor"), None),
            P(None, "tensor"),
            P("dp", None, "tensor"),
            P("dp", None, "tensor"),
            P("dp", "tensor"),
            P("dp", None),
            P(),
        ),
        out_specs=(
            P("dp", "tensor"),
            P(("dp", "tensor"), None),
            P("dp", None, "tensor"),
            P("dp", None, "tensor"),
        ),
        check_vma=False,
    )
```

```python
import functools

import jax
import jax.numpy as jnp
from jax import lax
from jax.experimental import pallas as pl
from jax.experimental.pallas import tpu as pltpu
from jax.sharding import PartitionSpec as P

adapter_scale = 2.0
bf16, f32 = jnp.bfloat16, jnp.float32
nt = (((1,), (1,)), ((), ()))
tn = (((0,), (0,)), ((), ()))
small_limit = 16 * 1024 * 1024
pieces_of_weight = 8
small_bytes = 8 * 1024 * 1024


def vmem():
    return pl.BlockSpec(memory_space=pltpu.VMEM)


def shape(dims, dtype):
    return jax.ShapeDtypeStruct(dims, dtype)


def call(
    body, name, outs, operands, specs, scratch=(), flops=0, moved=0, limit=small_limit, after=()
):
    count = len(operands)

    def run(*refs):
        body(*refs[:count], *refs[count + len(after) :])

    return list(
        pl.pallas_call(
            run,
            name=name,
            out_shape=outs,
            in_specs=specs + [pl.BlockSpec(memory_space=pl.ANY)] * len(after),
            out_specs=[vmem()] * len(outs),
            scratch_shapes=list(scratch),
            cost_estimate=pl.CostEstimate(flops=flops, bytes_accessed=moved, transcendentals=0),
            compiler_params=pltpu.CompilerParams(vmem_limit_bytes=limit),
        )(*operands, *after)
    )


def log2(n):
    return n.bit_length() - 1


def choose(refs, key):
    chosen = None
    for k in range(len(refs)):
        one = jnp.where(key == k, 1.0, 0.0).astype(bf16) * refs[k][...]
        chosen = one if chosen is None else chosen + one
    return chosen


def slot_kernel(*refs):
    owner, blocks = refs[0], refs[1:-3]
    upstream, slots, upstream_here = refs[-3:]
    upstream_here[...] = upstream[...]
    adapters = lax.broadcasted_iota(jnp.int32, owner.shape, 1)
    for k in range(len(blocks)):
        here = jnp.where(adapters == blocks[k][:1, :1], owner[...], 0)
        slot = jnp.sum(here, axis=1, keepdims=True)
        slots[k : k + 1, :] = jnp.broadcast_to(slot, (1, slots.shape[1]))


def base_kernel(upstream, weight, keep, give, rows_of):
    t = lax.axis_index("tensor")
    rows = keep.shape[1]
    half = keep.shape[0]
    step = weight.shape[0] // pieces_of_weight
    for n in range(half):
        for side in range(2):
            start = pl.multiple_of((2 * n + ((t & 1) ^ side)) * rows, rows)
            at = (side * half + n) * rows
            rows_of[at : at + rows, :] = upstream[pl.ds(start, rows), :]
    turned = rows_of[...].T
    for n in range(pieces_of_weight):
        part = jnp.dot(
            weight[n * step : (n + 1) * step, :], turned, preferred_element_type=f32
        ).T
        for m in range(half):
            keep[m, :, n * step : (n + 1) * step] = part[m * rows : (m + 1) * rows]
            at = (half + m) * rows
            give[m, :, n * step : (n + 1) * step] = part[at : at + rows]


def own_kernel(source, target):
    target[...] = source[...]


def stack_kernel(tokens, far, stack):
    stack[0] = tokens[...]
    stack[1] = far[...]


def pick_kernel(outer, inner, *refs):
    slots, column, found = refs[0], refs[1 : 1 + outer], refs[1 + outer :]
    o = lax.axis_index("dp") >> log2(inner)
    for k in range(inner):
        found[k][...] = choose(column, (slots[k : k + 1, :1] >> log2(inner)) ^ o)


def low_kernel(inner, parts, *refs):
    slots, found = refs[0], refs[1 : 1 + inner]
    tokens = refs[1 + inner : 3 + inner]
    upstream, both, chosen, columns, down = refs[3 + inner :]
    i = lax.axis_index("dp") & (inner - 1)
    t = lax.axis_index("tensor")
    cols = columns.shape[1]
    rows = columns.shape[0] // parts
    rank = chosen.shape[0] // 2
    chosen[...] = choose(found, (slots[:1, :1] & (inner - 1)) ^ i)
    down[...] = chosen[:rank, :]
    start = pl.multiple_of(t * cols, cols)
    for k in range(parts):
        at = pl.multiple_of((t ^ k) * rows, rows)
        columns[pl.ds(at, rows), :] = tokens[k & 1][k >> 1, :, pl.ds(start, cols)]
    both[:rank, :] = lax.dot_general(
        chosen[:rank, :], columns[...], nt, preferred_element_type=f32
    )
    both[rank:, :] = lax.dot_general(
        chosen[rank:, :], upstream[...], nt, preferred_element_type=f32
    )


def gradient_kernel(parts, *refs):
    totals = refs[:parts]
    columns, upstream, low, term = refs[parts:]
    rank = low.shape[0] // 2
    total = totals[0][...]
    for k in range(1, parts):
        total = total + totals[k][...]
    low[...] = total.astype(bf16)
    down_term = jnp.dot(low[rank:, :], columns[...], preferred_element_type=f32)
    up_term = jnp.dot(low[:rank, :], upstream[...], preferred_element_type=f32)
    term[:rank, :] = (adapter_scale * down_term).astype(bf16)
    term[rank:, :] = (adapter_scale * up_term).astype(bf16)


def route_kernel(outer, inner, *refs):
    slots, terms, parts = refs[0], refs[1 : 1 + inner], refs[1 + inner :]
    d = lax.axis_index("dp")
    for m in range(outer):
        target = d ^ (m * inner)
        part = None
        for k in range(inner):
            here = jnp.where(slots[k : k + 1, :1] == target, 1.0, 0.0).astype(bf16)
            one = here * terms[k][...]
            part = one if part is None else part + one
        parts[m][...] = part


def add_kernel(keep, got, low, chosen, sibling, hold, give, total, term):
    t = lax.axis_index("tensor")
    half, rows = keep.shape[0], keep.shape[1]
    rank, cols = sibling.shape
    high = t >> 1
    total[...] = keep[...] + got[...]
    for k, down in ((0, chosen), (1, sibling)):
        term[...] = adapter_scale * lax.dot_general(
            low[rank:, :], down[:rank, :], tn, preferred_element_type=f32
        )
        at = pl.multiple_of((t ^ k) * cols, cols)
        for n in range(half):
            start = pl.multiple_of((2 * n + (t & 1)) * rows, rows)
            total[n, :, pl.ds(at, cols)] += term[pl.ds(start, rows), :]
    hold[...] = total[high]
    give[...] = total[1 - high].astype(bf16)


def mixed_kernel(parts, *refs):
    tokens = refs[:2]
    weight, total, gathered = refs[2:]
    t = lax.axis_index("tensor")
    rows = tokens[0].shape[1]
    step = weight.shape[0] // pieces_of_weight
    for k in range(parts):
        at = pl.multiple_of((t ^ k) * rows, rows)
        gathered[pl.ds(at, rows), :] = tokens[k & 1][k >> 1]
    for n in range(pieces_of_weight):
        part = jnp.dot(
            gathered[:, n * step : (n + 1) * step],
            weight[n * step : (n + 1) * step, :],
            preferred_element_type=f32,
        )
        total[...] = part if n == 0 else total[...] + part


def finish_kernel(mixed, low, chosen, out):
    rank = low.shape[0] // 2
    term = lax.dot_general(low[:rank, :], chosen[rank:, :], tn, preferred_element_type=f32)
    out[...] = (mixed[...] + adapter_scale * term).astype(bf16)


def close_kernel(hold, got, out, done):
    out[...] = (hold[...] + got[...].astype(f32)).astype(bf16)
    done[...] = jnp.zeros(done.shape, f32)


def sum_kernel(*refs):
    parts, down, up = refs[:-2], refs[-2], refs[-1]
    rank = down.shape[1]
    total = parts[0][...].astype(f32)
    for part in parts[1:]:
        total = total + part[...].astype(f32)
    down[0] = total[:rank, :]
    up[0] = total[rank:, :]


def make_per_device(dp_size, tensor_size):
    inner = 1 << (log2(dp_size) // 2)
    outer = dp_size // inner
    half = tensor_size // 2

    def over_tensor(x, k):
        return lax.ppermute(x, "tensor", [(t, t ^ k) for t in range(tensor_size)])

    def over_inner(x, k):
        return lax.ppermute(x, "dp", [(d, d ^ k) for d in range(dp_size)])

    def over_outer(x, k):
        return lax.ppermute(x, "dp", [(d, d ^ (k * inner)) for d in range(dp_size)])

    def per_device(tokens, weight, down, up, upstream, adapter_per_block, owner):
        rank, cols = down.shape[1], down.shape[2]
        rows, width = tokens.shape
        length = upstream.shape[0]
        weight_bytes = weight.shape[0] * cols * 2
        flops = 2 * length * weight.shape[0] * cols

        mine = jnp.concatenate([down[0], up[0]], axis=0)
        column = [mine] + [over_outer(mine, k) for k in range(1, outer)]
        far = over_tensor(tokens, half)
        block = jnp.broadcast_to(adapter_per_block, (8, 128))
        blocks = [block] + [over_inner(block, k) for k in range(1, inner)]

        (column[0],) = call(
            own_kernel,
            "own",
            [shape(mine.shape, bf16)],
            (mine,),
            [vmem()],
            flops=8 * flops,
            after=(far,),
        )
        (stack,) = call(
            stack_kernel,
            "stack",
            [shape((half, rows, width), bf16)],
            (tokens, far),
            [vmem()] * 2,
            after=(column[0],),
        )
        (column[0],) = call(
            own_kernel,
            "again",
            [shape(mine.shape, bf16)],
            (column[0],),
            [vmem()],
            flops=8 * flops,
            after=(),
        )
        pieces = [stack, over_tensor(stack, 1)]
        slots, upstream_here = call(
            slot_kernel,
            "slots",
            [
                shape((inner, 128), jnp.int32),
                shape(upstream.shape, bf16),
            ],
            (owner.reshape(1, -1), *blocks, upstream),
            [vmem()] * (inner + 2),
            after=(column[0],),
        )
        found = call(
            functools.partial(pick_kernel, outer, inner),
            "pick",
            [shape((2 * rank, cols), bf16)] * inner,
            (slots, *column),
            [vmem()] * (1 + outer),
            flops=flops,
            moved=small_bytes,
        )
        keep, give = call(
            base_kernel,
            "base",
            [shape((half, rows, width), f32)] * 2,
            (upstream_here, weight),
            [vmem(), vmem()],
            [pltpu.VMEM((length, cols), bf16)],
            flops,
            weight_bytes,
            after=(found[0],),
        )
        found = [found[0]] + [over_inner(found[k], k) for k in range(1, inner)]

        both, chosen, columns, chosen_down = call(
            functools.partial(low_kernel, inner, tensor_size),
            "low",
            [
                shape((2 * rank, length), f32),
                shape((2 * rank, cols), bf16),
                shape((length, cols), bf16),
                shape((rank, cols), bf16),
            ],
            (slots, *found, *pieces, upstream_here),
            [vmem()] * (1 + inner + 2 + 1),
            flops=flops,
            moved=small_bytes,
        )
        (mixed,) = call(
            functools.partial(mixed_kernel, tensor_size),
            "mixed",
            [shape((length, cols), f32)],
            (*pieces, weight),
            [vmem()] * 3,
            [pltpu.VMEM((length, width), bf16)],
            flops,
            weight_bytes,
            after=(both,),
        )
        give, both = lax.optimization_barrier((give, both))
        got = over_tensor(give, 1)
        sibling = over_tensor(chosen_down, 1)
        totals = [both] + [over_tensor(both, k) for k in range(1, tensor_size)]

        low, term = call(
            functools.partial(gradient_kernel, tensor_size),
            "gradient",
            [shape((2 * rank, length), bf16), shape((2 * rank, cols), bf16)],
            (*totals, columns, upstream_here),
            [vmem()] * (tensor_size + 2),
            after=(mixed, sibling),
        )
        terms = [term] + [over_inner(term, k) for k in range(1, inner)]

        hold, give = call(
            add_kernel,
            "add",
            [shape((rows, width), f32), shape((rows, width), bf16)],
            (keep, got, low, chosen, sibling),
            [vmem()] * 5,
            [pltpu.VMEM((half, rows, width), f32), pltpu.VMEM((length, cols), f32)],
        )
        got = over_tensor(give, half)

        routed = call(
            functools.partial(route_kernel, outer, inner),
            "route",
            [shape((2 * rank, cols), bf16)] * outer,
            (slots, *terms),
            [vmem()] * (1 + inner),
            after=(give,),
        )
        parts = [routed[0]] + [over_outer(routed[m], m) for m in range(1, outer)]
        (mixed,) = call(
            finish_kernel,
            "finish",
            [shape((length, cols), bf16)],
            (mixed, low, chosen),
            [vmem()] * 3,
            flops=4 * flops,
            after=(routed[0],),
        )
        input_gradient, done = call(
            close_kernel,
            "close",
            [shape((rows, width), bf16), shape((8, 128), f32)],
            (hold, got),
            [vmem()] * 2,
        )
        down_gradient, up_gradient = call(
            sum_kernel,
            "sum",
            [shape(down.shape, f32)] * 2,
            parts[:1] + parts[:0:-1],
            [vmem()] * outer,
            after=(done,),
        )
        return mixed, input_gradient, down_gradient, up_gradient

    return per_device


def solution(mesh):
    return jax.shard_map(
        make_per_device(mesh.shape["dp"], mesh.shape["tensor"]),
        mesh=mesh,
        in_specs=(
            P(("dp", "tensor"), None),
            P(None, "tensor"),
            P("dp", None, "tensor"),
            P("dp", None, "tensor"),
            P("dp", "tensor"),
            P("dp", None),
            P(),
        ),
        out_specs=(
            P("dp", "tensor"),
            P(("dp", "tensor"), None),
            P("dp", None, "tensor"),
            P("dp", None, "tensor"),
        ),
        check_vma=False,
    )
```

```python
import functools

import jax
import jax.numpy as jnp
from jax import lax
from jax.experimental import pallas as pl
from jax.experimental.pallas import tpu as pltpu
from jax.sharding import PartitionSpec as P

adapter_scale = 2.0
bf16, f32 = jnp.bfloat16, jnp.float32
nt = (((1,), (1,)), ((), ()))
tn = (((0,), (0,)), ((), ()))
small_limit = 16 * 1024 * 1024
pieces_of_weight = 8
small_bytes = 8 * 1024 * 1024


def vmem():
    return pl.BlockSpec(memory_space=pltpu.VMEM)


def shape(dims, dtype):
    return jax.ShapeDtypeStruct(dims, dtype)


def call(
    body, name, outs, operands, specs, scratch=(), flops=0, moved=0, limit=small_limit, after=()
):
    count = len(operands)

    def run(*refs):
        body(*refs[:count], *refs[count + len(after) :])

    return list(
        pl.pallas_call(
            run,
            name=name,
            out_shape=outs,
            in_specs=specs + [pl.BlockSpec(memory_space=pl.ANY)] * len(after),
            out_specs=[vmem()] * len(outs),
            scratch_shapes=list(scratch),
            cost_estimate=pl.CostEstimate(flops=flops, bytes_accessed=moved, transcendentals=0),
            compiler_params=pltpu.CompilerParams(vmem_limit_bytes=limit),
        )(*operands, *after)
    )


def log2(n):
    return n.bit_length() - 1


def choose(refs, key):
    chosen = None
    for k in range(len(refs)):
        one = jnp.where(key == k, 1.0, 0.0).astype(bf16) * refs[k][...]
        chosen = one if chosen is None else chosen + one
    return chosen


def slot_kernel(*refs):
    owner, blocks = refs[0], refs[1:-3]
    upstream, slots, upstream_here = refs[-3:]
    upstream_here[...] = upstream[...]
    adapters = lax.broadcasted_iota(jnp.int32, owner.shape, 1)
    for k in range(len(blocks)):
        here = jnp.where(adapters == blocks[k][:1, :1], owner[...], 0)
        slot = jnp.sum(here, axis=1, keepdims=True)
        slots[k : k + 1, :] = jnp.broadcast_to(slot, (1, slots.shape[1]))


def base_kernel(upstream, weight, keep, give, rows_of):
    t = lax.axis_index("tensor")
    rows = keep.shape[1]
    half = keep.shape[0]
    step = weight.shape[0] // pieces_of_weight
    for n in range(half):
        for side in range(2):
            start = pl.multiple_of((2 * n + ((t & 1) ^ side)) * rows, rows)
            at = (side * half + n) * rows
            rows_of[at : at + rows, :] = upstream[pl.ds(start, rows), :]
    turned = rows_of[...].T
    for n in range(pieces_of_weight):
        part = jnp.dot(
            weight[n * step : (n + 1) * step, :], turned, preferred_element_type=f32
        ).T
        for m in range(half):
            keep[m, :, n * step : (n + 1) * step] = part[m * rows : (m + 1) * rows]
            at = (half + m) * rows
            give[m, :, n * step : (n + 1) * step] = part[at : at + rows]


def own_kernel(source, target):
    target[...] = source[...]


def stack_kernel(tokens, far, stack):
    stack[0] = tokens[...]
    stack[1] = far[...]


def pick_kernel(outer, inner, *refs):
    slots, column, found = refs[0], refs[1 : 1 + outer], refs[1 + outer :]
    o = lax.axis_index("dp") >> log2(inner)
    for k in range(inner):
        found[k][...] = choose(column, (slots[k : k + 1, :1] >> log2(inner)) ^ o)


def low_kernel(inner, parts, *refs):
    slots, found = refs[0], refs[1 : 1 + inner]
    tokens = refs[1 + inner : 3 + inner]
    upstream, both, chosen, columns, down = refs[3 + inner :]
    i = lax.axis_index("dp") & (inner - 1)
    t = lax.axis_index("tensor")
    cols = columns.shape[1]
    rows = columns.shape[0] // parts
    rank = chosen.shape[0] // 2
    chosen[...] = choose(found, (slots[:1, :1] & (inner - 1)) ^ i)
    down[...] = chosen[:rank, :]
    start = pl.multiple_of(t * cols, cols)
    for k in range(parts):
        at = pl.multiple_of((t ^ k) * rows, rows)
        columns[pl.ds(at, rows), :] = tokens[k & 1][k >> 1, :, pl.ds(start, cols)]
    both[:rank, :] = lax.dot_general(
        chosen[:rank, :], columns[...], nt, preferred_element_type=f32
    )
    both[rank:, :] = lax.dot_general(
        chosen[rank:, :], upstream[...], nt, preferred_element_type=f32
    )


def gradient_kernel(parts, *refs):
    totals = refs[:parts]
    columns, upstream, low, term = refs[parts:]
    rank = low.shape[0] // 2
    total = totals[0][...]
    for k in range(1, parts):
        total = total + totals[k][...]
    low[...] = total.astype(bf16)
    down_term = jnp.dot(low[rank:, :], columns[...], preferred_element_type=f32)
    up_term = jnp.dot(low[:rank, :], upstream[...], preferred_element_type=f32)
    term[:rank, :] = (adapter_scale * down_term).astype(bf16)
    term[rank:, :] = (adapter_scale * up_term).astype(bf16)


def route_kernel(outer, inner, *refs):
    slots, terms, parts = refs[0], refs[1 : 1 + inner], refs[1 + inner :]
    d = lax.axis_index("dp")
    for m in range(outer):
        target = d ^ (m * inner)
        part = None
        for k in range(inner):
            here = jnp.where(slots[k : k + 1, :1] == target, 1.0, 0.0).astype(bf16)
            one = here * terms[k][...]
            part = one if part is None else part + one
        parts[m][...] = part


def add_kernel(keep, got, low, chosen, sibling, hold, give, total, term):
    t = lax.axis_index("tensor")
    half, rows = keep.shape[0], keep.shape[1]
    rank, cols = sibling.shape
    high = t >> 1
    total[...] = keep[...] + got[...]
    for k, down in ((0, chosen), (1, sibling)):
        term[...] = adapter_scale * lax.dot_general(
            low[rank:, :], down[:rank, :], tn, preferred_element_type=f32
        )
        at = pl.multiple_of((t ^ k) * cols, cols)
        for n in range(half):
            start = pl.multiple_of((2 * n + (t & 1)) * rows, rows)
            total[n, :, pl.ds(at, cols)] += term[pl.ds(start, rows), :]
    hold[...] = total[high]
    give[...] = total[1 - high].astype(bf16)


def mixed_kernel(parts, *refs):
    tokens = refs[:2]
    weight, total, gathered = refs[2:]
    t = lax.axis_index("tensor")
    rows = tokens[0].shape[1]
    step = weight.shape[0] // pieces_of_weight
    for k in range(parts):
        at = pl.multiple_of((t ^ k) * rows, rows)
        gathered[pl.ds(at, rows), :] = tokens[k & 1][k >> 1]
    for n in range(pieces_of_weight):
        part = jnp.dot(
            gathered[:, n * step : (n + 1) * step],
            weight[n * step : (n + 1) * step, :],
            preferred_element_type=f32,
        )
        total[...] = part if n == 0 else total[...] + part


def finish_kernel(mixed, low, chosen, out):
    rank = low.shape[0] // 2
    term = lax.dot_general(low[:rank, :], chosen[rank:, :], tn, preferred_element_type=f32)
    out[...] = (mixed[...] + adapter_scale * term).astype(bf16)


def close_kernel(hold, got, out, done):
    out[...] = (hold[...] + got[...].astype(f32)).astype(bf16)
    done[...] = jnp.zeros(done.shape, f32)


def sum_kernel(*refs):
    parts, down, up = refs[:-2], refs[-2], refs[-1]
    rank = down.shape[1]
    total = parts[0][...].astype(f32)
    for part in parts[1:]:
        total = total + part[...].astype(f32)
    down[0] = total[:rank, :]
    up[0] = total[rank:, :]


def make_per_device(dp_size, tensor_size):
    inner = 1 << (log2(dp_size) // 2)
    outer = dp_size // inner
    half = tensor_size // 2

    def over_tensor(x, k):
        return lax.ppermute(x, "tensor", [(t, t ^ k) for t in range(tensor_size)])

    def over_inner(x, k):
        return lax.ppermute(x, "dp", [(d, d ^ k) for d in range(dp_size)])

    def over_outer(x, k):
        return lax.ppermute(x, "dp", [(d, d ^ (k * inner)) for d in range(dp_size)])

    def per_device(tokens, weight, down, up, upstream, adapter_per_block, owner):
        rank, cols = down.shape[1], down.shape[2]
        rows, width = tokens.shape
        length = upstream.shape[0]
        weight_bytes = weight.shape[0] * cols * 2
        flops = 2 * length * weight.shape[0] * cols

        mine = jnp.concatenate([down[0], up[0]], axis=0)
        column = [mine] + [over_outer(mine, k) for k in range(1, outer)]
        far = over_tensor(tokens, half)
        block = jnp.broadcast_to(adapter_per_block, (8, 128))
        blocks = [block] + [over_inner(block, k) for k in range(1, inner)]

        (column[0],) = call(
            own_kernel,
            "own",
            [shape(mine.shape, bf16)],
            (mine,),
            [vmem()],
            flops=8 * flops,
            after=(far,),
        )
        (stack,) = call(
            stack_kernel,
            "stack",
            [shape((half, rows, width), bf16)],
            (tokens, far),
            [vmem()] * 2,
            after=(column[0],),
        )
        (column[0],) = call(
            own_kernel,
            "again",
            [shape(mine.shape, bf16)],
            (column[0],),
            [vmem()],
            flops=8 * flops,
            after=(),
        )
        pieces = [stack, over_tensor(stack, 1)]
        slots, upstream_here = call(
            slot_kernel,
            "slots",
            [
                shape((inner, 128), jnp.int32),
                shape(upstream.shape, bf16),
            ],
            (owner.reshape(1, -1), *blocks, upstream),
            [vmem()] * (inner + 2),
            after=(column[0],),
        )
        found = call(
            functools.partial(pick_kernel, outer, inner),
            "pick",
            [shape((2 * rank, cols), bf16)] * inner,
            (slots, *column),
            [vmem()] * (1 + outer),
            flops=flops,
            moved=small_bytes,
            after=(pieces[1],),
        )
        keep, give = call(
            base_kernel,
            "base",
            [shape((half, rows, width), f32)] * 2,
            (upstream_here, weight),
            [vmem(), vmem()],
            [pltpu.VMEM((length, cols), bf16)],
            flops,
            weight_bytes,
            after=(found[0],),
        )
        found = [found[0]] + [over_inner(found[k], k) for k in range(1, inner)]
        give, *found[1:] = lax.optimization_barrier((give, *found[1:]))
        got = over_tensor(give, 1)

        both, chosen, columns, chosen_down = call(
            functools.partial(low_kernel, inner, tensor_size),
            "low",
            [
                shape((2 * rank, length), f32),
                shape((2 * rank, cols), bf16),
                shape((length, cols), bf16),
                shape((rank, cols), bf16),
            ],
            (slots, *found, *pieces, upstream_here),
            [vmem()] * (1 + inner + 2 + 1),
            flops=flops,
            moved=small_bytes,
        )
        (mixed,) = call(
            functools.partial(mixed_kernel, tensor_size),
            "mixed",
            [shape((length, cols), f32)],
            (*pieces, weight),
            [vmem()] * 3,
            [pltpu.VMEM((length, width), bf16)],
            flops,
            weight_bytes,
            after=(both,),
        )
        sibling = over_tensor(chosen_down, 1)
        totals = [both] + [over_tensor(both, k) for k in range(1, tensor_size)]

        low, term = call(
            functools.partial(gradient_kernel, tensor_size),
            "gradient",
            [shape((2 * rank, length), bf16), shape((2 * rank, cols), bf16)],
            (*totals, columns, upstream_here),
            [vmem()] * (tensor_size + 2),
            after=(mixed, sibling),
        )
        terms = [term] + [over_inner(term, k) for k in range(1, inner)]

        hold, give = call(
            add_kernel,
            "add",
            [shape((rows, width), f32), shape((rows, width), bf16)],
            (keep, got, low, chosen, sibling),
            [vmem()] * 5,
            [pltpu.VMEM((half, rows, width), f32), pltpu.VMEM((length, cols), f32)],
        )
        got = over_tensor(give, half)

        routed = call(
            functools.partial(route_kernel, outer, inner),
            "route",
            [shape((2 * rank, cols), bf16)] * outer,
            (slots, *terms),
            [vmem()] * (1 + inner),
            after=(give,),
        )
        parts = [routed[0]] + [over_outer(routed[m], m) for m in range(1, outer)]
        (mixed,) = call(
            finish_kernel,
            "finish",
            [shape((length, cols), bf16)],
            (mixed, low, chosen),
            [vmem()] * 3,
            flops=4 * flops,
            after=(routed[0],),
        )
        input_gradient, done = call(
            close_kernel,
            "close",
            [shape((rows, width), bf16), shape((8, 128), f32)],
            (hold, got),
            [vmem()] * 2,
        )
        down_gradient, up_gradient = call(
            sum_kernel,
            "sum",
            [shape(down.shape, f32)] * 2,
            parts[:1] + parts[:0:-1],
            [vmem()] * outer,
            after=(done,),
        )
        return mixed, input_gradient, down_gradient, up_gradient

    return per_device


def solution(mesh):
    return jax.shard_map(
        make_per_device(mesh.shape["dp"], mesh.shape["tensor"]),
        mesh=mesh,
        in_specs=(
            P(("dp", "tensor"), None),
            P(None, "tensor"),
            P("dp", None, "tensor"),
            P("dp", None, "tensor"),
            P("dp", "tensor"),
            P("dp", None),
            P(),
        ),
        out_specs=(
            P("dp", "tensor"),
            P(("dp", "tensor"), None),
            P("dp", None, "tensor"),
            P("dp", None, "tensor"),
        ),
        check_vma=False,
    )
```
